256 devices in a mesh: ia: 4 (over z_lo), ja: 8 (over y, core), ka: 8 (over x, z_hi).
Axes of the slice: x: 4, y: 4, z: 8 (z_hi: 2, z_lo: 4; z = z_hi * 4 + z_lo), core: 2. Of those that a mesh axis runs over, the one named last changes fastest.
Arguments:
- features: bfloat16 [768, 6144], P('ia', ('ka', 'ja')), may hold values from -6 to 6
- in_weight: bfloat16 [6144, 24576], P(('ka', 'ia'), 'ja'), may hold values from -0.078125 to 0.078125
- out_weight: bfloat16 [24576, 6144], P(('ja', 'ia'), 'ka'), may hold values from -0.0390625 to 0.0390625
- cotangent: bfloat16 [768, 6144], P('ia', ('ka', 'ja')), may hold values from -1.5 to 1.5
Outputs:
- layer_out: bfloat16 [768, 6144], P('ia', ('ka', 'ja'))
- feature_grad: bfloat16 [768, 6144], P('ia', ('ka', 'ja'))
- in_weight_grad: bfloat16 [6144, 24576], P(('ka', 'ia'), 'ja')
- out_weight_grad: bfloat16 [24576, 6144], P(('ja', 'ia'), 'ka')
The draws below stay inside these ranges and needn't reach their ends.
All inputs are finite; a program needn't handle non-finite values.
Results may differ from the reference program's by a relative error of at most 0.028.
Values may be sent and summed in bfloat16 or wider, within the bound.
A program may use at most 64 MiB of HBM per device.

```python
import jax
import jax.numpy as jnp
from jax import lax

D = 6144
FF = 24576
ROWS = 192
TOKENS = 768
N_IA = 4


def steps_of(own_key, dims, cuts, least, largest):
    factor_of, own = 1.0, jax.random.fold_in(own_key, 6)
    for position, blocks in cuts:
        draws = jnp.exp(jax.random.uniform(jax.random.fold_in(own, position), (blocks,), jnp.float32, least / len(cuts), largest / len(cuts)))
        factor_of = factor_of * jnp.repeat(draws, dims[position] // blocks).reshape([-1 if axis == position else 1 for axis in range(len(dims))])
    return factor_of


def noise(rng, shape, width, bound, pieces=(), held_as=jnp.bfloat16):
    result = width * jax.random.normal(rng, shape, jnp.float32)
    if pieces:
        result = result * steps_of(rng, shape, pieces, -0.22, 0.18)
    return jnp.clip(result, -bound, bound).astype(held_as)


def setup_inputs(seed: int = 0) -> dict:
    streams_of = jax.random.split(jax.random.key(seed), 5)
    return {
        "features": noise(streams_of[0], (TOKENS, D), 1.0, 6.0, ((0, 4), (1, 64))),
        "in_weight": noise(streams_of[1], (D, FF), D ** -0.5, 0.078125, ((0, 32), (1, 8))),
        "out_weight": noise(streams_of[2], (FF, D), FF ** -0.5, 0.0390625, ((0, 32), (1, 8))),
        "cotangent": noise(streams_of[3], (TOKENS, D), 0.25, 1.5, ((0, 4), (1, 64))),
    }


GELU_SCALE = 0.7978845608028654


def gelu_value(hidden):
    inner = GELU_SCALE * (hidden + 0.044715 * hidden * hidden * hidden)
    return 0.5 * hidden * (1.0 + jnp.tanh(inner))


def gelu_slope(hidden):
    tangent = jnp.tanh(GELU_SCALE * (hidden + 0.044715 * hidden * hidden * hidden))
    return 0.5 * (1.0 + tangent) + 0.5 * hidden * (1.0 - tangent * tangent) * GELU_SCALE * (1.0 + 3.0 * 0.044715 * hidden * hidden)


def transposed(left, right):
    return lax.dot_general(left, right, (((1,), (1,)), ((), ())), preferred_element_type=jnp.float32)


def inner_rows(left, right):
    return lax.dot_general(left, right, (((0,), (0,)), ((), ())), preferred_element_type=jnp.float32)


def reference(features, in_weight, out_weight, cotangent):
    pre = jnp.dot(features, in_weight, preferred_element_type=jnp.float32)
    active = gelu_value(pre).astype(jnp.bfloat16)
    layer_out = jnp.dot(active, out_weight, preferred_element_type=jnp.float32).astype(jnp.bfloat16)
    grad_active = transposed(cotangent, out_weight)
    grad_pre = (grad_active * gelu_slope(pre)).astype(jnp.bfloat16)
    feature_grad = transposed(grad_pre, in_weight).astype(jnp.bfloat16)
    in_sum = jnp.zeros(in_weight.shape, jnp.float32)
    out_sum = jnp.zeros(out_weight.shape, jnp.float32)
    for group in range(N_IA):
        low = group * ROWS
        term_in = inner_rows(features[low:low + ROWS], grad_pre[low:low + ROWS]).astype(jnp.bfloat16)
        in_sum = in_sum + lax.optimization_barrier(term_in).astype(jnp.float32)
        term_out = inner_rows(active[low:low + ROWS], cotangent[low:low + ROWS]).astype(jnp.bfloat16)
        out_sum = out_sum + lax.optimization_barrier(term_out).astype(jnp.float32)
    return layer_out, feature_grad, in_sum.astype(jnp.bfloat16), out_sum.astype(jnp.bfloat16)
```

```python
import functools

import jax
import jax.numpy as jnp
from jax import lax
from jax.experimental import pallas as pl
from jax.experimental.pallas import tpu as pltpu
from jax.sharding import PartitionSpec as P

GELU_SCALE = 0.7978845608028654
BF = jnp.bfloat16
F32 = jnp.float32
MESH = pl.DeviceIdType.MESH

NI, NY, NC, NX, NZ = 4, 4, 2, 4, 2
NJ = NY * NC
ROWS, FEAT, BLOCK = 192, 96, 768
TOKENS = NI * ROWS
PACK, PR, PW = 4, 48, 384
NH = 3
HC = BLOCK // NH
HALF = ROWS // 2


def dot(left, right, contract):
    return lax.dot_general(left, right, (contract, ((), ())), preferred_element_type=F32)


NN = ((1,), (0,))
NT = ((1,), (1,))
TN = ((0,), (0,))


def kernel(
    feat_ref, cot_ref, w1_ref, w2_hbm,
    out_ref, fgrad_ref, dw1_ref, dw2_ref,
    gx, gc, xs, cs, w1r, w2, gpart, ppart, grecv, precv, gsum, psum, gsend, psend, gz, pz,
    act, gp, dwb, dw2b, pk, rc, s1, ry, s2, rz, send_sem, recv_sem, local_sem,
):
    ia, ja, ka = lax.axis_index("ia"), lax.axis_index("ja"), lax.axis_index("ka")
    yy, cc, xx, zz = ja // NC, lax.rem(ja, NC), ka // NZ, lax.rem(ka, NZ)

    def at_i(d):
        i = lax.rem(ia + d, NI)
        return i, (i, ja, ka)

    def at_y(d):
        y = lax.rem(yy + d, NY)
        return y, (ia, y * NC + cc, ka)

    def at_x(d):
        x = lax.rem(xx + d, NX)
        return x, (ia, ja, x * NZ + zz)

    core = (ia, yy * NC + 1 - cc, ka)
    zpair = (ia, ja, xx * NZ + 1 - zz)

    barrier = pltpu.get_barrier_semaphore()
    peers = [at_i(d)[1] for d in (1, 2, 3)] + [at_y(d)[1] for d in (1, 2, 3)]
    peers += [at_x(d)[1] for d in (1, 2, 3)] + [core, zpair]
    for peer in peers:
        pl.semaphore_signal(barrier, inc=1, device_id=peer, device_id_type=MESH)

    count = [0, 0]
    sent, local = [], []

    def remote(src, dst, device):
        n = count[0]
        count[0] += 1
        copy = pltpu.make_async_remote_copy(
            src_ref=src, dst_ref=dst, send_sem=send_sem.at[n], recv_sem=recv_sem.at[n],
            device_id=device, device_id_type=MESH,
        )
        copy.start()
        sent.append(copy)
        return copy

    def nearby(src, dst):
        n = count[1]
        count[1] += 1
        copy = pltpu.make_async_copy(src, dst, local_sem.at[n])
        copy.start()
        return copy

    def cols(index, width):
        return pl.ds(pl.multiple_of(index * width, width), width)

    w2_copy = nearby(w2_hbm, w2)
    w1_own = [nearby(w1_ref.at[:, cols(ia * NH + h, HC)], w1r.at[h, cols(ia, ROWS)]) for h in range(NH)]
    gc[ja, ia] = cot_ref[...]
    gx[ja, ia] = feat_ref[...]
    pl.semaphore_wait(barrier, len(peers))

    z_c = [remote(cot_ref, gc.at[ja, ia], at_i(d)[1]) for d in (1, 2, 3)]
    z_x = [remote(feat_ref, gx.at[ja, ia], at_i(d)[1]) for d in (1, 2, 3)]
    y_copies, core_copies = [], []
    for buf, arrivals in ((gc, z_c), (gx, z_x)):
        for copy in arrivals:
            copy.wait_recv()
        y_copies.append([remote(buf.at[ja], buf.at[ja], at_y(d)[1]) for d in (1, 2, 3)])
        core_copies.append([remote(buf.at[ja], buf.at[ja], core)])

    w1_in = []
    for h in range(NH):
        w1_in.append([])
        for d in (1, 2, 3):
            i, device = at_i(d)
            w1_in[h].append(remote(w1_ref.at[:, cols(i * NH + h, HC)], w1r.at[h, cols(ia, ROWS)], device))

    def unpack(buf, dst):
        def body(i, carry):
            for g in range(PACK):
                row = pl.multiple_of(i * ROWS + g * PR, PR)
                dst[pl.ds(row, PR), :] = jnp.concatenate(
                    [buf[j, i, :, g * FEAT:(g + 1) * FEAT] for j in range(NJ)], axis=1
                )
            return carry
        lax.fori_loop(0, NI, body, 0)

    def finish_gather(n, buf, dst):
        for d, copy in zip((1, 2, 3), y_copies[n]):
            copy.wait_recv()
            j = lax.rem(yy + NY - d, NY) * NC + cc
            core_copies[n].append(remote(buf.at[j], buf.at[j], core))
        for copy in core_copies[n]:
            copy.wait_recv()
        unpack(buf, dst)

    finish_gather(0, gc, cs)
    w2_copy.wait()
    for h in range(NH):
        def body(t, carry):
            rows = cols(t, ROWS)
            gpart[h, rows] = dot(cs[rows], w2[h * HC:(h + 1) * HC], NT).astype(BF)
            return carry
        lax.fori_loop(0, NX, body, 0)
    g_x = []
    for d in (1, 2, 3):
        x, device = at_x(d)
        g_x.append(remote(gpart.at[:, cols(x, ROWS)], grecv.at[d - 1], device))

    finish_gather(1, gx, xs)
    p_x = []
    for h in range(NH):
        w1_own[h].wait()
        for copy in w1_in[h]:
            copy.wait_recv()

        def body(t, carry):
            rows = cols(t, ROWS)
            ppart[h, rows] = dot(xs[rows], w1r[h], NN).astype(BF)
            return carry
        lax.fori_loop(0, NX, body, 0)
        p_x.append([])
        for d in (1, 2, 3):
            x, device = at_x(d)
            p_x[h].append(remote(ppart.at[h, cols(x, ROWS)], precv.at[h, d - 1], device))

    for copy in g_x:
        copy.wait_recv()
    for h in range(NH):
        total = gpart[h, cols(xx, ROWS)].astype(F32)
        for d in range(3):
            total += grecv[d, h].astype(F32)
        for half in range(2):
            gsum[half, h] = total[half * HALF:(half + 1) * HALF]
            gsend[half, h] = total[half * HALF:(half + 1) * HALF].astype(BF)
    g_z = remote(gsend.at[1 - zz], gz, zpair)
    p_z = []
    for h in range(NH):
        for copy in p_x[h]:
            copy.wait_recv()
        total = ppart[h, cols(xx, ROWS)].astype(F32)
        for d in range(3):
            total += precv[h, d].astype(F32)
        for half in range(2):
            psum[h, half] = total[half * HALF:(half + 1) * HALF]
            psend[h, half] = total[half * HALF:(half + 1) * HALF].astype(BF)
        p_z.append(remote(psend.at[h, 1 - zz], pz.at[h], zpair))

    g_z.wait_recv()
    mine = pl.ds(pl.multiple_of(xx * ROWS + zz * HALF, HALF), HALF)
    theirs = pl.ds(pl.multiple_of(xx * ROWS + (1 - zz) * HALF, HALF), HALF)
    pair, direct, passed = {}, {}, {}
    for h in range(NH):
        p_z[h].wait_recv()
        pre = psum[h, zz] + pz[h].astype(F32)
        grad = gsum[zz, h] + gz[h].astype(F32)
        square = pre * pre
        tangent = jnp.tanh(GELU_SCALE * (pre + 0.044715 * square * pre))
        act[h, mine] = (0.5 * pre * (1.0 + tangent)).astype(BF)
        slope = 0.5 * (1.0 + tangent) + 0.5 * pre * (1.0 - tangent * tangent) * GELU_SCALE * (
            1.0 + 3.0 * 0.044715 * square
        )
        gp[h, mine] = (grad * slope).astype(BF)
        for n, buf in ((0, gp), (1, act)):
            pair[n, h] = remote(buf.at[h, mine], buf.at[h, mine], zpair)
            direct[n, h] = [remote(buf.at[h, mine], buf.at[h, mine], at_x(d)[1]) for d in (1, 2, 3)]
    for n, buf in ((0, gp), (1, act)):
        for h in range(NH):
            pair[n, h].wait_recv()
            passed[n, h] = [remote(buf.at[h, theirs], buf.at[h, theirs], at_x(d)[1]) for d in (1, 2, 3)]

    dw1_in, dw1_own = [], []
    for h in range(NH):
        for copy in direct[0, h] + passed[0, h]:
            copy.wait_recv()

        def body(t, carry):
            dwb[h, cols(t, 256)] = dot(xs[:, cols(t, 256)], gp[h], TN).astype(BF)
            return carry
        lax.fori_loop(0, BLOCK // 256, body, 0)
        for d in (1, 2, 3):
            i, device = at_i(d)
            dw1_in.append(remote(dwb.at[h, cols(i, ROWS)], dw1_ref.at[:, cols(ia * NH + h, HC)], device))
        dw1_own.append(nearby(dwb.at[h, cols(ia, ROWS)], dw1_ref.at[:, cols(ia * NH + h, HC)]))

    def pack(n, value, i):
        value = value.astype(BF)
        for j in range(NJ):
            pk[n, j, i] = jnp.concatenate(
                [value[g * PR:(g + 1) * PR, j * FEAT:(j + 1) * FEAT] for g in range(PACK)], axis=1
            )

    def body(i, carry):
        rows = cols(i, ROWS)
        total = dot(gp[0, rows], w1r[0], NT)
        for h in range(1, NH):
            total += dot(gp[h, rows], w1r[h], NT)
        pack(0, total, i)
        return carry
    lax.fori_loop(0, NI, body, 0)

    def to_core(n):
        return [
            remote(pk.at[n, y * NC + 1 - cc], rc.at[n, y], core) for y in range(NY)
        ]
    core_in = {0: to_core(0)}
    for h in range(NH):
        for copy in direct[1, h] + passed[1, h]:
            copy.wait_recv()

    def body(i, carry):
        rows = cols(i, ROWS)
        total = dot(act[0, rows], w2[0:HC], NN)
        for h in range(1, NH):
            total += dot(act[h, rows], w2[h * HC:(h + 1) * HC], NN)
        pack(1, total, i)
        return carry
    lax.fori_loop(0, NI, body, 0)
    core_in[1] = to_core(1)

    y_in = {}
    for n in range(2):
        for y in range(NY):
            core_in[n][y].wait_recv()
            s1[n, y] = (pk[n, y * NC + cc].astype(F32) + rc[n, y].astype(F32)).astype(BF)
        y_in[n] = []
        for d in (1, 2, 3):
            y, device = at_y(d)
            y_in[n].append(remote(s1.at[n, y], ry.at[n, d - 1], device))

    for h in range(NH):
        dw2b[h * HC:(h + 1) * HC] = dot(act[h], cs[...], TN).astype(BF)
    dw2_copy = nearby(dw2b, dw2_ref)

    z_in = {}
    for n in range(2):
        for copy in y_in[n]:
            copy.wait_recv()
        total = s1[n, yy].astype(F32)
        for d in range(3):
            total += ry[n, d].astype(F32)
        s2[n] = total.astype(BF)
        z_in[n] = []
        for d in (1, 2, 3):
            i, device = at_i(d)
            z_in[n].append(remote(s2.at[n, i], rz.at[n, d - 1], device))
    for n, ref in ((0, fgrad_ref), (1, out_ref)):
        for copy in z_in[n]:
            copy.wait_recv()
        total = s2[n, ia].astype(F32)
        for d in range(3):
            total += rz[n, d].astype(F32)
        ref[...] = total.astype(BF)

    for copy in dw1_in:
        copy.wait_recv()
    for copy in dw1_own + [dw2_copy]:
        copy.wait()
    for copy in sent:
        copy.wait_send()


def packed(piece):
    return piece.reshape(PACK, PR, FEAT).transpose(1, 0, 2).reshape(PR, PW)


def unpacked(piece):
    return piece.reshape(PR, PACK, FEAT).transpose(1, 0, 2).reshape(ROWS, FEAT)


def local(features, in_weight, out_weight, cotangent):
    vmem = pl.BlockSpec(memory_space=pltpu.VMEM)
    hbm = pl.BlockSpec(memory_space=pl.ANY)
    buf = lambda *shape: pltpu.VMEM(shape, BF)
    wide = lambda *shape: pltpu.VMEM(shape, F32)
    out, fgrad, dw1, dw2 = pl.pallas_call(
        kernel,
        out_shape=(
            jax.ShapeDtypeStruct((PR, PW), BF),
            jax.ShapeDtypeStruct((PR, PW), BF),
            jax.ShapeDtypeStruct((ROWS, NI * BLOCK), BF),
            jax.ShapeDtypeStruct((BLOCK, BLOCK), BF),
        ),
        in_specs=[vmem, vmem, hbm, hbm],
        out_specs=(vmem, vmem, hbm, hbm),
        scratch_shapes=[
            buf(NJ, NI, PR, PW), buf(NJ, NI, PR, PW),
            buf(TOKENS, BLOCK), buf(TOKENS, BLOCK),
            buf(NH, BLOCK, HC), buf(BLOCK, BLOCK),
            buf(NH, TOKENS, HC), buf(NH, TOKENS, HC),
            buf(3, NH, ROWS, HC), buf(NH, 3, ROWS, HC),
            wide(2, NH, HALF, HC), wide(NH, 2, HALF, HC),
            buf(2, NH, HALF, HC), buf(NH, 2, HALF, HC),
            buf(NH, HALF, HC), buf(NH, HALF, HC),
            buf(NH, TOKENS, HC), buf(NH, TOKENS, HC),
            buf(NH, BLOCK, HC), buf(BLOCK, BLOCK),
            buf(2, NJ, NI, PR, PW), buf(2, NY, NI, PR, PW),
            buf(2, NY, NI, PR, PW), buf(2, 3, NI, PR, PW),
            buf(2, NI, PR, PW), buf(2, 3, PR, PW),
            pltpu.SemaphoreType.DMA((128,)),
            pltpu.SemaphoreType.DMA((128,)),
            pltpu.SemaphoreType.DMA((12,)),
        ],
        name="block",
        compiler_params=pltpu.CompilerParams(
            collective_id=0, has_side_effects=True, vmem_limit_bytes=56 * 2**20
        ),
        cost_estimate=pl.CostEstimate(
            flops=12 * BLOCK**3, bytes_accessed=8 * BLOCK * BLOCK, transcendentals=HALF * BLOCK
        ),
    )(packed(features), packed(cotangent), in_weight, out_weight)
    return unpacked(out), unpacked(fgrad), dw1, dw2


def solution(mesh):
    placed = (
        P("ia", ("ka", "ja")),
        P(("ka", "ia"), "ja"),
        P(("ja", "ia"), "ka"),
        P("ia", ("ka", "ja")),
    )
    return jax.shard_map(
        local,
        mesh=mesh,
        in_specs=placed,
        out_specs=(
            P("ia", ("ka", "ja")),
            P("ia", ("ka", "ja")),
            P(("ka", "ia"), "ja"),
            P(("ja", "ia"), "ka"),
        ),
        check_vma=False,
    )
```

```python
import functools

import jax
import jax.numpy as jnp
from jax import lax
from jax.experimental import pallas as pl
from jax.experimental.pallas import tpu as pltpu
from jax.sharding import PartitionSpec as P

GELU_SCALE = 0.7978845608028654
BF = jnp.bfloat16
F32 = jnp.float32
MESH = pl.DeviceIdType.MESH

NI, NY, NC, NX, NZ = 4, 4, 2, 4, 2
NJ = NY * NC
RING = NZ * NI
ROWS, FEAT, BLOCK = 192, 96, 768
TOKENS = NI * ROWS
PACK, PR, PW = 4, 48, 384
NH = 3
HC = BLOCK // NH


def dot(left, right, contract):
    return lax.dot_general(left, right, (contract, ((), ())), preferred_element_type=F32)


NN = ((1,), (0,))
NT = ((1,), (1,))
TN = ((0,), (0,))


def guarded(when, action):
    if when is None:
        action()
    else:
        @pl.when(when)
        def _():
            action()


class Transfer:
    def __init__(self, copy, when, arrives):
        self.copy, self.when, self.arrives = copy, when, arrives

    def start(self):
        guarded(self.when, self.copy.start)

    def wait_send(self):
        guarded(self.when, self.copy.wait_send)

    def wait_recv(self):
        guarded(self.arrives, self.copy.wait_recv)


def kernel(
    feat_hbm, cot_hbm, w1_hbm, w2_hbm,
    out_ref, fgrad_ref, dw1_ref, dw2_ref,
    raw, own, gx, gc, xs, xt, cs, w1, w1r, w2, gpart, grecv, gsum, gz, ppart, precv, psum, pz,
    act, gp, dwb, dw2b,
    pk0, rc0, s0, ry0, t0, rb0, rz0, pk1, rc1, s1, ry1, t1, rz1,
    send_sem, recv_sem, local_sem,
):
    ia, ja, ka = lax.axis_index("ia"), lax.axis_index("ja"), lax.axis_index("ka")
    yy, cc, xx, zz = ja // NC, lax.rem(ja, NC), ka // NZ, lax.rem(ka, NZ)
    ring = zz * NI + ia

    def at_i(d):
        i = lax.rem(ia + d, NI)
        return i, (i, ja, ka)

    def at_z(d):
        z = lax.rem(ring + d, RING)
        return z, (lax.rem(z, NI), ja, xx * NZ + z // NI)

    def at_y(d):
        y = lax.rem(yy + d, NY)
        return y, (ia, y * NC + cc, ka)

    def at_x(d):
        x = lax.rem(xx + d, NX)
        return x, (ia, ja, x * NZ + zz)

    core = (ia, yy * NC + 1 - cc, ka)
    zpair = at_z(NI)[1]

    barrier = pltpu.get_barrier_semaphore()
    peers = [at_z(d)[1] for d in range(1, RING)] + [at_y(d)[1] for d in (1, 2, 3)]
    peers += [at_x(d)[1] for d in (1, 2, 3)] + [core]
    for peer in peers:
        pl.semaphore_signal(barrier, inc=1, device_id=peer, device_id_type=MESH)

    count = [0, 0]
    sent = []

    def remote(src, dst, device, when=None, arrives=None):
        n = count[0]
        count[0] += 1
        copy = Transfer(pltpu.make_async_remote_copy(
            src_ref=src, dst_ref=dst, send_sem=send_sem.at[n], recv_sem=recv_sem.at[n],
            device_id=device, device_id_type=MESH,
        ), when, arrives)
        copy.start()
        sent.append(copy)
        return copy

    def nearby(src, dst):
        n = count[1]
        count[1] += 1
        copy = pltpu.make_async_copy(src, dst, local_sem.at[n])
        copy.start()
        return copy

    def cols(index, width):
        return pl.ds(pl.multiple_of(index * width, width), width)

    raw_copies = [nearby(cot_hbm, raw.at[0]), nearby(feat_hbm, raw.at[1])]
    w1_copy = nearby(w1_hbm, w1)
    w2_copy = nearby(w2_hbm, w2)
    for n in range(2):
        raw_copies[n].wait()
        own[n] = jnp.concatenate([raw[n, g * PR:(g + 1) * PR] for g in range(PACK)], axis=1)
    gc[ja, ia] = own[0]
    gx[ja, zz, ia] = own[1]
    pl.semaphore_wait(barrier, len(peers))

    def split(y):
        return lax.rem(y - ia + NI, NI) == 2

    def high(y, c):
        near = lax.rem(y - ia + NI + 1, NI) - 1
        return lax.rem(ring + RING + near - NI * c * ((near + 1) // 3), RING) // NI

    def in_reach(z, row):
        return lax.rem(z - row + 2 + RING, RING) <= 4

    def to_y(src, dst):
        return [remote(src, dst, at_y(d)[1]) for d in (1, 2, 3)]

    z_c = [remote(own.at[0], gc.at[ja, ia], at_i(d)[1]) for d in (1, 2, 3)]
    c_y = [to_y(own.at[0], gc.at[ja, ia])]
    for d, copy in zip((1, 2, 3), z_c):
        copy.wait_recv()
        i = lax.rem(ia + NI - d, NI)
        c_y.append(to_y(gc.at[ja, i], gc.at[ja, i]))
    c_core = [remote(gc.at[ja], gc.at[ja], core)]
    x_z = []
    for d in range(1, RING):
        z, device = at_z(d)
        source = lax.rem(ring + RING - d, RING)
        x_z.append(remote(
            own.at[1], gx.at[ja, zz, ia], device,
            in_reach(z, zz * NI + yy), in_reach(ring, source // NI * NI + yy),
        ))
    for d in (1, 2, 3):
        for copies in c_y:
            copies[d - 1].wait_recv()
        j = lax.rem(yy + NY - d, NY) * NC + cc
        c_core.append(remote(gc.at[j], gc.at[j], core))

    w1_copy.wait()
    w1_in = []
    for h in range(NH):
        w1_in.append([])
        for d in (1, 7, 6 - 4 * cc):
            z, device = at_z(d)
            place = cols(lax.rem(z, NI) * NH + h, HC)
            w1_in[h].append(remote(w1.at[:, place], w1r.at[h, cols(ia, ROWS)], device))
        w1r[h, cols(ia, ROWS)] = w1[:, cols(ia * NH + h, HC)]

    for copy in x_z:
        copy.wait_recv()
    here = high(yy, cc)
    x_y = to_y(gx.at[ja, here], gx.at[ja, here])
    x_b = []
    for d in (1, 2, 3):
        source = lax.rem(yy + NY - d, NY)
        x_b.append(remote(
            gx.at[ja, 1 - here], gx.at[ja, 1 - here], at_y(d)[1], split(yy), split(source)
        ))
    there = high(yy, 1 - cc)
    x_core = [remote(gx.at[ja, there], gx.at[ja, there], core)]

    def unpack(dst, rows_of):
        def body(i, carry):
            for g in range(PACK):
                row = pl.multiple_of(i * ROWS + g * PR, PR)
                dst[pl.ds(row, PR), :] = jnp.concatenate(
                    [rows_of(j, i)[:, g * FEAT:(g + 1) * FEAT] for j in range(NJ)], axis=1
                )
            return carry
        lax.fori_loop(0, NI, body, 0)

    for copy in c_core:
        copy.wait_recv()
    unpack(cs, lambda j, i: gc[j, i])
    w2_copy.wait()

    def over_x(part, landing, h):
        copies = []
        for d in (1, 2, 3):
            x, device = at_x(d)
            copies.append(remote(part.at[h, cols(x, ROWS)], landing.at[h, d - 1], device))
        return copies

    def grad_part(h):
        def body(t, carry):
            rows = cols(t, ROWS)
            gpart[h, rows] = dot(cs[rows], w2[h * HC:(h + 1) * HC], NT).astype(BF)
            return carry
        lax.fori_loop(0, NX, body, 0)
        return over_x(gpart, grecv, h)

    g_x = [grad_part(0), grad_part(1)]

    for d in (1, 2, 3):
        y = lax.rem(yy + NY - d, NY)
        x_y[d - 1].wait_recv()
        x_b[d - 1].wait_recv()
        there = high(y, 1 - cc)
        j = y * NC + cc
        x_core.append(remote(gx.at[j, there], gx.at[j, there], core))
    for copy in x_core:
        copy.wait_recv()
    unpack(xs, lambda j, i: gx[j, high(j // NC, cc), i])

    p_x = []
    for h in range(NH):
        for copy in w1_in[h]:
            copy.wait_recv()

        def body(t, carry):
            rows = cols(t, ROWS)
            ppart[h, rows] = dot(xs[rows], w1r[h], NN).astype(BF)
            return carry
        lax.fori_loop(0, NX, body, 0)
        p_x.append(over_x(ppart, precv, h))
    g_x.append(grad_part(2))

    def body(t, carry):
        xt[cols(t, 256)] = xs[:, cols(t, 256)].T
        return carry
    lax.fori_loop(0, BLOCK // 256, body, 0)

    mine = cols(xx, ROWS)

    def over_pair(part, landing, copies, total_ref, other, h):
        for copy in copies[h]:
            copy.wait_recv()
        total = part[h, mine].astype(F32)
        for d in range(3):
            total += landing[h, d].astype(F32)
        total_ref[h] = total.astype(BF)
        return remote(total_ref.at[h], other.at[h], zpair)

    g_z = [over_pair(gpart, grecv, g_x, gsum, gz, h) for h in range(2)]

    gp_x, act_x = [], []

    def activate(h, pair):
        pair.wait_recv()
        pre = psum[h].astype(F32) + pz[h].astype(F32)
        square = pre * pre
        tangent = jnp.tanh(GELU_SCALE * (pre + 0.044715 * square * pre))
        act[h, mine] = (0.5 * pre * (1.0 + tangent)).astype(BF)
        slope = 0.5 * (1.0 + tangent) + 0.5 * pre * (1.0 - tangent * tangent) * GELU_SCALE * (
            1.0 + 3.0 * 0.044715 * square
        )
        g_z[h].wait_recv()
        grad = gsum[h].astype(F32) + gz[h].astype(F32)
        gp[h, mine] = (grad * slope).astype(BF)
        gp_x.append([remote(gp.at[h, mine], gp.at[h, mine], at_x(d)[1]) for d in (1, 2, 3)])

    def send_act(h):
        act_x.append([remote(act.at[h, mine], act.at[h, mine], at_x(d)[1]) for d in (1, 2, 3)])

    p_z = [over_pair(ppart, precv, p_x, psum, pz, 0), over_pair(ppart, precv, p_x, psum, pz, 1)]
    activate(0, p_z[0])
    p_z.append(over_pair(ppart, precv, p_x, psum, pz, 2))
    g_z.append(over_pair(gpart, grecv, g_x, gsum, gz, 2))
    activate(1, p_z[1])
    send_act(0)
    activate(2, p_z[2])
    send_act(1)
    send_act(2)

    dw1_in, dw1_own = [], []
    for h in range(NH):
        for copy in gp_x[h]:
            copy.wait_recv()

        def body(t, carry):
            dwb[h, cols(t, 256)] = dot(xt[cols(t, 256)], gp[h], NN).astype(BF)
            return carry
        lax.fori_loop(0, BLOCK // 256, body, 0)
        place = cols(ia * NH + h, HC)
        for d in (1, 7, 2 + 4 * cc):
            z, device = at_z(d)
            dw1_in.append(remote(dwb.at[h, cols(lax.rem(z, NI), ROWS)], dw1_ref.at[:, place], device))
        dw1_own.append(nearby(dwb.at[h, cols(ia, ROWS)], dw1_ref.at[:, place]))

    def packed(value, j):
        return jnp.concatenate(
            [value[g * PR:(g + 1) * PR, j * FEAT:(j + 1) * FEAT] for g in range(PACK)], axis=1
        )

    def body(i, carry):
        rows = cols(i, ROWS)
        left = jnp.concatenate([gp[h, rows] for h in range(NH)], axis=1)
        right = jnp.concatenate([w1r[h] for h in range(NH)], axis=1)
        total = dot(left, right, NT).astype(BF)
        for j in range(NJ):
            pk0[j, i] = packed(total, j)
        return carry
    lax.fori_loop(0, NI, body, 0)
    def to_core(part, landing):
        copies = []
        for d in range(NY):
            y = lax.rem(yy + d, NY)
            copies.append(remote(part.at[y * NC + 1 - cc], landing.at[y], core))
        return copies

    core0 = to_core(pk0, rc0)

    y0, b0 = [], []
    for d in (1, 2, 3, 0):
        y, device = at_y(d)
        core0[d].wait_recv()
        s0[y] = pk0[y * NC + cc]

        @pl.when(jnp.logical_not(split(y)))
        def _():
            s0[y] = (pk0[y * NC + cc].astype(F32) + rc0[y].astype(F32)).astype(BF)
        if d:
            y0.append(remote(s0.at[y], ry0.at[d - 1], device))
            b0.append(remote(rc0.at[y], rb0.at[d - 1], device, split(y), split(yy)))

    for copies in act_x:
        for copy in copies:
            copy.wait_recv()

    def body(i, carry):
        rows = cols(i, ROWS)
        left = jnp.concatenate([act[h, rows] for h in range(NH)], axis=1)
        total = dot(left, w2[...], NN).astype(BF)
        for j in range(NJ):
            pk1[j, i] = packed(total, j)
        return carry
    lax.fori_loop(0, NI, body, 0)
    core1 = to_core(pk1, rc1)
    y1 = []
    for d in (1, 2, 3, 0):
        y, device = at_y(d)
        core1[d].wait_recv()
        s1[y] = (pk1[y * NC + cc].astype(F32) + rc1[y].astype(F32)).astype(BF)
        if d:
            y1.append(remote(s1.at[y], ry1.at[d - 1], device))

    for h in range(NH):
        dw2b[h * HC:(h + 1) * HC] = dot(act[h], cs[...], TN).astype(BF)
    dw2_copy = nearby(dw2b, dw2_ref)

    for copy in y0:
        copy.wait_recv()
    total = s0[yy].astype(F32)
    for d in range(3):
        total += ry0[d].astype(F32)
    t0[1 - here] = jnp.zeros((NI, PR, PW), BF)
    t0[here] = total.astype(BF)

    for copy in b0:
        copy.wait_recv()

    @pl.when(split(yy))
    def _():
        total = rc0[yy].astype(F32)
        for d in range(3):
            total += rb0[d].astype(F32)
        t0[1 - here] = total.astype(BF)

    z0 = []
    for d in range(1, RING):
        z, device = at_z(d)
        source = lax.rem(ring + RING - d, RING)
        z0.append(remote(
            t0.at[z // NI, lax.rem(z, NI)], rz0.at[d - 1], device,
            in_reach(ring, z // NI * NI + yy), in_reach(source, zz * NI + yy),
        ))

    for copy in y1:
        copy.wait_recv()
    total = s1[yy].astype(F32)
    for d in range(3):
        total += ry1[d].astype(F32)
    t1[...] = total.astype(BF)
    z1 = []
    for d in (1, 2, 3):
        i, device = at_i(d)
        z1.append(remote(t1.at[i], rz1.at[d - 1], device))

    def finish(total, ref):
        total = total.astype(BF)
        for g in range(PACK):
            ref[g * PR:(g + 1) * PR, :] = total[:, g * FEAT:(g + 1) * FEAT]

    total = t0[zz, ia].astype(F32)
    for n, copy in enumerate(z0):
        copy.wait_recv()

        @pl.when(jnp.logical_not(copy.arrives))
        def _():
            rz0[n] = jnp.zeros((PR, PW), BF)
        total += rz0[n].astype(F32)
    finish(total, fgrad_ref)

    total = t1[ia].astype(F32)
    for n, copy in enumerate(z1):
        copy.wait_recv()
        total += rz1[n].astype(F32)
    finish(total, out_ref)

    for copy in dw1_in:
        copy.wait_recv()
    for copy in dw1_own + [dw2_copy]:
        copy.wait()
    for copy in sent:
        copy.wait_send()


def handover(*refs):
    sources, targets, staging, sem = refs[:4], refs[4:8], refs[8:12], refs[12]
    pieces = []
    for source, stage, target in zip(sources, staging, targets):
        parts = 4 if source.shape[1] > BLOCK // 2 else 1
        rows = source.shape[0] // parts
        for n in range(parts):
            at = pl.ds(n * rows, rows)
            pieces.append((source.at[at], stage.at[at], target.at[at]))
    loads = [pltpu.make_async_copy(p[0], p[1], sem.at[0, n]) for n, p in enumerate(pieces)]
    stores = [pltpu.make_async_copy(p[1], p[2], sem.at[1, n]) for n, p in enumerate(pieces)]
    for load in loads:
        load.start()
    for load, store in zip(loads, stores):
        load.wait()
        store.start()
    for store in stores:
        store.wait()


def local(features, in_weight, out_weight, cotangent):
    vmem = pl.BlockSpec(memory_space=pltpu.VMEM)
    hbm = pl.BlockSpec(memory_space=pl.ANY)
    buf = lambda *shape: pltpu.VMEM(shape, BF)
    wide = lambda *shape: pltpu.VMEM(shape, F32)
    results = pl.pallas_call(
        kernel,
        out_shape=(
            jax.ShapeDtypeStruct((ROWS, FEAT), BF),
            jax.ShapeDtypeStruct((ROWS, FEAT), BF),
            jax.ShapeDtypeStruct((ROWS, NI * BLOCK), BF),
            jax.ShapeDtypeStruct((BLOCK, BLOCK), BF),
        ),
        in_specs=[hbm] * 4,
        out_specs=(vmem, vmem, hbm, hbm),
        scratch_shapes=[
            buf(2, ROWS, FEAT), buf(2, PR, PW), buf(NJ, NZ, NI, PR, PW), buf(NJ, NI, PR, PW),
            buf(TOKENS, BLOCK), buf(BLOCK, TOKENS), buf(TOKENS, BLOCK),
            buf(ROWS, NI * BLOCK), buf(NH, BLOCK, HC), buf(BLOCK, BLOCK),
            buf(NH, TOKENS, HC), buf(NH, 3, ROWS, HC), buf(NH, ROWS, HC), buf(NH, ROWS, HC),
            buf(NH, TOKENS, HC), buf(NH, 3, ROWS, HC), buf(NH, ROWS, HC), buf(NH, ROWS, HC),
            buf(NH, TOKENS, HC), buf(NH, TOKENS, HC),
            buf(NH, BLOCK, HC), buf(BLOCK, BLOCK),
            buf(NJ, NI, PR, PW), buf(NY, NI, PR, PW), buf(NY, NI, PR, PW),
            buf(3, NI, PR, PW), buf(NZ, NI, PR, PW), buf(3, NI, PR, PW), buf(RING - 1, PR, PW),
            buf(NJ, NI, PR, PW), buf(NY, NI, PR, PW), buf(NY, NI, PR, PW),
            buf(3, NI, PR, PW), buf(NI, PR, PW), buf(3, PR, PW),
            pltpu.SemaphoreType.DMA((124,)),
            pltpu.SemaphoreType.DMA((124,)),
            pltpu.SemaphoreType.DMA((8,)),
        ],
        name="block",
        compiler_params=pltpu.CompilerParams(
            collective_id=0, has_side_effects=True, vmem_limit_bytes=60 * 2**20
        ),
        cost_estimate=pl.CostEstimate(
            flops=12 * BLOCK**3, bytes_accessed=8 * BLOCK * BLOCK, transcendentals=ROWS * BLOCK
        ),
    )(features, cotangent, in_weight, out_weight)
    return pl.pallas_call(
        handover,
        out_shape=tuple(jax.ShapeDtypeStruct(r.shape, r.dtype) for r in results),
        in_specs=[hbm] * 4,
        out_specs=(hbm,) * 4,
        scratch_shapes=[pltpu.VMEM(r.shape, r.dtype) for r in results] + [pltpu.SemaphoreType.DMA((2, 10))],
        name="handover",
        compiler_params=pltpu.CompilerParams(vmem_limit_bytes=60 * 2**20),
    )(*results)


def solution(mesh):
    placed = (
        P("ia", ("ka", "ja")),
        P(("ka", "ia"), "ja"),
        P(("ja", "ia"), "ka"),
        P("ia", ("ka", "ja")),
    )
    return jax.shard_map(
        local,
        mesh=mesh,
        in_specs=placed,
        out_specs=(
            P("ia", ("ka", "ja")),
            P("ia", ("ka", "ja")),
            P(("ka", "ia"), "ja"),
            P(("ja", "ia"), "ka"),
        ),
        check_vma=False,
    )
```

```python
import functools

import jax
import jax.numpy as jnp
from jax import lax
from jax.experimental import pallas as pl
from jax.experimental.pallas import tpu as pltpu
from jax.sharding import PartitionSpec as P

GELU_SCALE = 0.7978845608028654
BF = jnp.bfloat16
F32 = jnp.float32
MESH = pl.DeviceIdType.MESH

NI, NY, NC, NX, NZ = 4, 4, 2, 4, 2
NJ = NY * NC
RING = NZ * NI
ROWS, FEAT, BLOCK = 192, 96, 768
TOKENS = NI * ROWS
PACK, PR, PW = 4, 48, 384
NH = 3
HC = BLOCK // NH


def dot(left, right, contract):
    return lax.dot_general(left, right, (contract, ((), ())), preferred_element_type=F32)


NN = ((1,), (0,))
NT = ((1,), (1,))
TN = ((0,), (0,))


def guarded(when, action):
    if when is None:
        action()
    else:
        @pl.when(when)
        def _():
            action()


class Transfer:
    def __init__(self, copy, when, arrives):
        self.copy, self.when, self.arrives = copy, when, arrives

    def start(self):
        guarded(self.when, self.copy.start)

    def wait_send(self):
        guarded(self.when, self.copy.wait_send)

    def wait_recv(self):
        guarded(self.arrives, self.copy.wait_recv)


def kernel(
    feat_hbm, cot_hbm, w1_hbm, w2_hbm,
    out_ref, fgrad_ref, dw1_ref, dw2_ref,
    raw, own, gx, gc, xs, xt, cs, w1, w1r, w2, gpart, grecv, gpass, gsum, gz,
    ppart, precv, ppass, psum, pz,
    act, gp, dwb, dw2b,
    pk0, rc0, s0, ry0, t0, rz0, pk1, rc1, s1, ry1, t1, rz1,
    send_sem, recv_sem, local_sem,
):
    ia, ja, ka = lax.axis_index("ia"), lax.axis_index("ja"), lax.axis_index("ka")
    yy, cc, xx, zz = ja // NC, lax.rem(ja, NC), ka // NZ, lax.rem(ka, NZ)
    ring = zz * NI + ia

    def at_i(d):
        i = lax.rem(ia + d, NI)
        return i, (i, ja, ka)

    def at_z(d):
        z = lax.rem(ring + d, RING)
        return z, (lax.rem(z, NI), ja, xx * NZ + z // NI)

    def at_y(d):
        y = lax.rem(yy + d, NY)
        return y, (ia, y * NC + cc, ka)

    def at_x(x):
        return (ia, ja, x * NZ + zz)

    even, odd = xx + 1 - 2 * lax.rem(xx, 2), NX - 1 - xx
    first, second = even + cc * (odd - even), odd + cc * (even - odd)
    across = lax.rem(xx + 2, NX)

    core = (ia, yy * NC + 1 - cc, ka)
    zpair = at_z(NI)[1]

    barrier = pltpu.get_barrier_semaphore()
    peers = [at_z(d)[1] for d in range(1, RING)] + [at_y(d)[1] for d in (1, 2, 3)]
    peers += [at_x(first), at_x(second), core]
    for peer in peers:
        pl.semaphore_signal(barrier, inc=1, device_id=peer, device_id_type=MESH)

    count = [0, 0]
    sent = []

    def remote(src, dst, device, when=None, arrives=None):
        n = count[0]
        count[0] += 1
        copy = Transfer(pltpu.make_async_remote_copy(
            src_ref=src, dst_ref=dst, send_sem=send_sem.at[n], recv_sem=recv_sem.at[n],
            device_id=device, device_id_type=MESH,
        ), when, arrives)
        copy.start()
        sent.append(copy)
        return copy

    def nearby(src, dst):
        n = count[1]
        count[1] += 1
        copy = pltpu.make_async_copy(src, dst, local_sem.at[n])
        copy.start()
        return copy

    def cols(index, width):
        return pl.ds(pl.multiple_of(index * width, width), width)

    raw_copies = [nearby(cot_hbm, raw.at[0]), nearby(feat_hbm, raw.at[1])]
    w1_copy = nearby(w1_hbm, w1)
    w2_copy = nearby(w2_hbm, w2)
    for n in range(2):
        raw_copies[n].wait()
        own[n] = jnp.concatenate([raw[n, g * PR:(g + 1) * PR] for g in range(PACK)], axis=1)
    gc[ja, ia] = own[0]
    gx[ja, zz, ia] = own[1]
    pl.semaphore_wait(barrier, len(peers))

    odd_z = lax.rem(ia, 2)

    def high(y):
        near = lax.rem(y - ia + NI + 1, NI) - 1
        return lax.rem(ring + RING + near - NI * odd_z * ((near + 1) // 3), RING) // NI

    def in_reach(z, row):
        return lax.rem(row - z + 1 + lax.rem(z, 2) + RING, RING) <= 3

    def to_y(src, dst):
        return [remote(src, dst, at_y(d)[1]) for d in (1, 2, 3)]

    z_c = [remote(own.at[0], gc.at[ja, ia], at_i(d)[1]) for d in (1, 2, 3)]
    c_y = [to_y(own.at[0], gc.at[ja, ia])]
    for d, copy in zip((1, 2, 3), z_c):
        copy.wait_recv()
        i = lax.rem(ia + NI - d, NI)
        c_y.append(to_y(gc.at[ja, i], gc.at[ja, i]))
    c_core = [remote(gc.at[ja], gc.at[ja], core)]
    x_z = []
    for d in range(1, RING):
        z, device = at_z(d)
        source = lax.rem(ring + RING - d, RING)
        x_z.append(remote(
            own.at[1], gx.at[ja, zz, ia], device,
            in_reach(z, zz * NI + yy), in_reach(ring, source // NI * NI + yy),
        ))
    w1_copy.wait()
    w1_in = []
    for h in range(NH):
        w1_in.append([])
        for d in (1, 7, 6 - 4 * odd_z):
            z, device = at_z(d)
            place = cols(lax.rem(z, NI) * NH + h, HC)
            w1_in[h].append(remote(w1.at[:, place], w1r.at[h, cols(ia, ROWS)], device))
        w1r[h, cols(ia, ROWS)] = w1[:, cols(ia * NH + h, HC)]

    for d in (1, 2, 3):
        for copies in c_y:
            copies[d - 1].wait_recv()
        j = lax.rem(yy + NY - d, NY) * NC + cc
        c_core.append(remote(gc.at[j], gc.at[j], core))

    for copy in x_z:
        copy.wait_recv()
    here = high(yy)
    x_y = to_y(gx.at[ja, here], gx.at[ja, here])
    x_core = [remote(gx.at[ja, here], gx.at[ja, here], core)]

    def unpack(dst, rows_of):
        def body(i, carry):
            for g in range(PACK):
                row = pl.multiple_of(i * ROWS + g * PR, PR)
                dst[pl.ds(row, PR), :] = jnp.concatenate(
                    [rows_of(j, i)[:, g * FEAT:(g + 1) * FEAT] for j in range(NJ)], axis=1
                )
            return carry
        lax.fori_loop(0, NI, body, 0)

    for copy in c_core:
        copy.wait_recv()
    unpack(cs, lambda j, i: gc[j, i])
    w2_copy.wait()

    mine = cols(xx, ROWS)

    def sum_first(part, landing, h):
        return [
            remote(part.at[h, cols(x, ROWS)], landing.at[h, n], at_x(first))
            for n, x in ((1, across), (0, first))
        ]

    def sum_second(part, landing, passing, copies, h):
        copies[0].wait_recv()
        passing[h] = (part[h, cols(second, ROWS)].astype(F32) + landing[h, 1].astype(F32)).astype(BF)
        copies.append(remote(passing.at[h], landing.at[h, 2], at_x(second)))

    def sum_pair(part, landing, total_ref, other, copies, h):
        copies[1].wait_recv()
        copies[2].wait_recv()
        total = part[h, mine].astype(F32) + landing[h, 0].astype(F32) + landing[h, 2].astype(F32)
        total_ref[h] = total.astype(BF)
        return remote(total_ref.at[h], other.at[h], zpair)

    def grad_part(h):
        def body(t, carry):
            rows = cols(t, ROWS)
            gpart[h, rows] = dot(cs[rows], w2[h * HC:(h + 1) * HC], NT).astype(BF)
            return carry
        lax.fori_loop(0, NX, body, 0)
        return sum_first(gpart, grecv, h)

    g_x = [grad_part(h) for h in range(NH)]

    def grad_second(h):
        sum_second(gpart, grecv, gpass, g_x[h], h)

    def grad_pair(h):
        return sum_pair(gpart, grecv, gsum, gz, g_x[h], h)

    for d in (1, 2, 3):
        y = lax.rem(yy + NY - d, NY)
        x_y[d - 1].wait_recv()
        there = high(y)
        j = y * NC + cc
        x_core.append(remote(gx.at[j, there], gx.at[j, there], core))
    grad_second(0)
    for copy in x_core:
        copy.wait_recv()
    unpack(xs, lambda j, i: gx[j, high(j // NC), i])

    p_x = []
    for h in range(NH):
        for copy in w1_in[h]:
            copy.wait_recv()

        def body(t, carry):
            rows = cols(t, ROWS)
            ppart[h, rows] = dot(xs[rows], w1r[h], NN).astype(BF)
            return carry
        lax.fori_loop(0, NX, body, 0)
        p_x.append(sum_first(ppart, precv, h))
        if h < 2:
            grad_second(h + 1)
    g_z = [grad_pair(h) for h in range(NH)]

    def body(t, carry):
        xt[cols(t, 256)] = xs[:, cols(t, 256)].T
        return carry
    lax.fori_loop(0, BLOCK // 256, body, 0)

    p_z = []

    def pre_second(h):
        sum_second(ppart, precv, ppass, p_x[h], h)

    def pre_pair(h):
        p_z.append(sum_pair(ppart, precv, psum, pz, p_x[h], h))

    pre_second(0)
    pre_second(1)
    pre_pair(0)
    pre_second(2)
    pre_pair(1)
    pre_pair(2)

    class Gather:
        def __init__(self, ref, at):
            self.ref, self.at = ref, at
            self.own = [self.send(xx, x) for x in (first, second)]

        def send(self, rows, x):
            piece = self.ref.at[self.at, cols(rows, ROWS)]
            return remote(piece, piece, at_x(x))

        def pass_on(self):
            self.own[0].wait_recv()
            self.own.append(self.send(first, second))

        def finish(self):
            for copy in self.own[1:]:
                copy.wait_recv()

    gp_x, act_x = [], []

    def activate(h):
        p_z[h].wait_recv()
        pre = psum[h].astype(F32) + pz[h].astype(F32)
        square = pre * pre
        tangent = jnp.tanh(GELU_SCALE * (pre + 0.044715 * square * pre))
        act[h, mine] = (0.5 * pre * (1.0 + tangent)).astype(BF)
        slope = 0.5 * (1.0 + tangent) + 0.5 * pre * (1.0 - tangent * tangent) * GELU_SCALE * (
            1.0 + 3.0 * 0.044715 * square
        )
        g_z[h].wait_recv()
        grad = gsum[h].astype(F32) + gz[h].astype(F32)
        gp[h, mine] = (grad * slope).astype(BF)
        gp_x.append(Gather(gp, h))

    dw1_in, dw1_own = [], []

    def in_weight_grad(h):
        def body(t, carry):
            dwb[h, cols(t, 256)] = dot(xt[cols(t, 256)], gp[h], NN).astype(BF)
            return carry
        lax.fori_loop(0, BLOCK // 256, body, 0)
        place = cols(ia * NH + h, HC)
        for d in (1, 7, 2 + 4 * odd_z):
            z, device = at_z(d)
            dw1_in.append(remote(dwb.at[h, cols(lax.rem(z, NI), ROWS)], dw1_ref.at[:, place], device))
        dw1_own.append(nearby(dwb.at[h, cols(ia, ROWS)], dw1_ref.at[:, place]))

    activate(0)
    activate(1)
    gp_x[0].pass_on()
    activate(2)
    gp_x[1].pass_on()
    act_x += [Gather(act, 0), Gather(act, 1)]
    gp_x[2].pass_on()
    act_x.append(Gather(act, 2))
    act_x[0].pass_on()
    act_x[1].pass_on()
    gp_x[0].finish()
    in_weight_grad(0)
    gp_x[1].finish()
    gp_x[2].finish()
    act_x[2].pass_on()

    def packed(value, j):
        return jnp.concatenate(
            [value[g * PR:(g + 1) * PR, j * FEAT:(j + 1) * FEAT] for g in range(PACK)], axis=1
        )

    def body(i, carry):
        rows = cols(i, ROWS)
        left = jnp.concatenate([gp[h, rows] for h in range(NH)], axis=1)
        right = jnp.concatenate([w1r[h] for h in range(NH)], axis=1)
        total = dot(left, right, NT).astype(BF)
        for j in range(NJ):
            pk0[j, i] = packed(total, j)
        return carry
    lax.fori_loop(0, NI, body, 0)
    def to_core(part, landing):
        copies = []
        for d in range(NY):
            y = lax.rem(yy + d, NY)
            copies.append(remote(part.at[y * NC + 1 - cc], landing.at[y], core))
        return copies

    core0 = to_core(pk0, rc0)
    in_weight_grad(1)

    def to_rows(partial, arrived, copies, summed, landing):
        started = []
        for d in (1, 2, 3, 0):
            y, device = at_y(d)
            copies[d].wait_recv()
            summed[y] = (partial[y * NC + cc].astype(F32) + arrived[y].astype(F32)).astype(BF)
            if d:
                started.append(remote(summed.at[y], landing.at[d - 1], device))
        return started

    y0 = to_rows(pk0, rc0, core0, s0, ry0)

    for gather in act_x:
        gather.finish()

    def body(i, carry):
        rows = cols(i, ROWS)
        left = jnp.concatenate([act[h, rows] for h in range(NH)], axis=1)
        total = dot(left, w2[...], NN).astype(BF)
        for j in range(NJ):
            pk1[j, i] = packed(total, j)
        return carry
    lax.fori_loop(0, NI, body, 0)
    core1 = to_core(pk1, rc1)
    in_weight_grad(2)
    y1 = to_rows(pk1, rc1, core1, s1, ry1)

    for h in range(NH):
        dw2b[h * HC:(h + 1) * HC] = dot(act[h], cs[...], TN).astype(BF)
    dw2_copy = nearby(dw2b, dw2_ref)

    for copy in y0:
        copy.wait_recv()
    total = s0[yy].astype(F32)
    for d in range(3):
        total += ry0[d].astype(F32)
    t0[...] = total.astype(BF)
    z0 = []
    for d in range(1, RING):
        z, device = at_z(d)
        source = lax.rem(ring + RING - d, RING)
        z0.append(remote(
            t0.at[lax.rem(z, NI)], rz0.at[d - 1], device,
            in_reach(ring, z // NI * NI + yy), in_reach(source, zz * NI + yy),
        ))

    for copy in y1:
        copy.wait_recv()
    total = s1[yy].astype(F32)
    for d in range(3):
        total += ry1[d].astype(F32)
    t1[...] = total.astype(BF)
    z1 = []
    for d in (1, 2, 3):
        i, device = at_i(d)
        z1.append(remote(t1.at[i], rz1.at[d - 1], device))

    def finish(total, ref):
        total = total.astype(BF)
        for g in range(PACK):
            ref[g * PR:(g + 1) * PR, :] = total[:, g * FEAT:(g + 1) * FEAT]

    total = jnp.where(here == zz, t0[ia].astype(F32), 0.0)
    for n, copy in enumerate(z0):
        copy.wait_recv()

        @pl.when(jnp.logical_not(copy.arrives))
        def _():
            rz0[n] = jnp.zeros((PR, PW), BF)
        total += rz0[n].astype(F32)
    finish(total, fgrad_ref)

    total = t1[ia].astype(F32)
    for n, copy in enumerate(z1):
        copy.wait_recv()
        total += rz1[n].astype(F32)
    finish(total, out_ref)

    for copy in dw1_in:
        copy.wait_recv()
    for copy in dw1_own + [dw2_copy]:
        copy.wait()
    for copy in sent:
        copy.wait_send()


def handover(*refs):
    sources, targets, staging, sem = refs[:4], refs[4:8], refs[8:12], refs[12]
    pieces = []
    for source, stage, target in zip(sources, staging, targets):
        parts = 4 if source.shape[1] > BLOCK // 2 else 1
        rows = source.shape[0] // parts
        for n in range(parts):
            at = pl.ds(n * rows, rows)
            pieces.append((source.at[at], stage.at[at], target.at[at]))
    loads = [pltpu.make_async_copy(p[0], p[1], sem.at[0, n]) for n, p in enumerate(pieces)]
    stores = [pltpu.make_async_copy(p[1], p[2], sem.at[1, n]) for n, p in enumerate(pieces)]
    for load in loads:
        load.start()
    for load, store in zip(loads, stores):
        load.wait()
        store.start()
    for store in stores:
        store.wait()


def local(features, in_weight, out_weight, cotangent):
    vmem = pl.BlockSpec(memory_space=pltpu.VMEM)
    hbm = pl.BlockSpec(memory_space=pl.ANY)
    buf = lambda *shape: pltpu.VMEM(shape, BF)
    wide = lambda *shape: pltpu.VMEM(shape, F32)
    results = pl.pallas_call(
        kernel,
        out_shape=(
            jax.ShapeDtypeStruct((ROWS, FEAT), BF),
            jax.ShapeDtypeStruct((ROWS, FEAT), BF),
            jax.ShapeDtypeStruct((ROWS, NI * BLOCK), BF),
            jax.ShapeDtypeStruct((BLOCK, BLOCK), BF),
        ),
        in_specs=[hbm] * 4,
        out_specs=(vmem, vmem, hbm, hbm),
        scratch_shapes=[
            buf(2, ROWS, FEAT), buf(2, PR, PW), buf(NJ, NZ, NI, PR, PW), buf(NJ, NI, PR, PW),
            buf(TOKENS, BLOCK), buf(BLOCK, TOKENS), buf(TOKENS, BLOCK),
            buf(ROWS, NI * BLOCK), buf(NH, BLOCK, HC), buf(BLOCK, BLOCK),
            buf(NH, TOKENS, HC), buf(NH, 3, ROWS, HC), buf(NH, ROWS, HC),
            buf(NH, ROWS, HC), buf(NH, ROWS, HC),
            buf(NH, TOKENS, HC), buf(NH, 3, ROWS, HC), buf(NH, ROWS, HC),
            buf(NH, ROWS, HC), buf(NH, ROWS, HC),
            buf(NH, TOKENS, HC), buf(NH, TOKENS, HC),
            buf(NH, BLOCK, HC), buf(BLOCK, BLOCK),
            buf(NJ, NI, PR, PW), buf(NY, NI, PR, PW), buf(NY, NI, PR, PW),
            buf(3, NI, PR, PW), buf(NI, PR, PW), buf(RING - 1, PR, PW),
            buf(NJ, NI, PR, PW), buf(NY, NI, PR, PW), buf(NY, NI, PR, PW),
            buf(3, NI, PR, PW), buf(NI, PR, PW), buf(3, PR, PW),
            pltpu.SemaphoreType.DMA((118,)),
            pltpu.SemaphoreType.DMA((118,)),
            pltpu.SemaphoreType.DMA((8,)),
        ],
        name="block",
        compiler_params=pltpu.CompilerParams(
            collective_id=0, has_side_effects=True, vmem_limit_bytes=60 * 2**20
        ),
        cost_estimate=pl.CostEstimate(
            flops=12 * BLOCK**3, bytes_accessed=8 * BLOCK * BLOCK, transcendentals=ROWS * BLOCK
        ),
    )(features, cotangent, in_weight, out_weight)
    return pl.pallas_call(
        handover,
        out_shape=tuple(jax.ShapeDtypeStruct(r.shape, r.dtype) for r in results),
        in_specs=[hbm] * 4,
        out_specs=(hbm,) * 4,
        scratch_shapes=[pltpu.VMEM(r.shape, r.dtype) for r in results] + [pltpu.SemaphoreType.DMA((2, 10))],
        name="handover",
        compiler_params=pltpu.CompilerParams(vmem_limit_bytes=60 * 2**20),
    )(*results)


def solution(mesh):
    placed = (
        P("ia", ("ka", "ja")),
        P(("ka", "ia"), "ja"),
        P(("ja", "ia"), "ka"),
        P("ia", ("ka", "ja")),
    )
    return jax.shard_map(
        local,
        mesh=mesh,
        in_specs=placed,
        out_specs=(
            P("ia", ("ka", "ja")),
            P("ia", ("ka", "ja")),
            P(("ka", "ia"), "ja"),
            P(("ja", "ia"), "ka"),
        ),
        check_vma=False,
    )
```

```python
import functools

import jax
import jax.numpy as jnp
from jax import lax
from jax.experimental import pallas as pl
from jax.experimental.pallas import tpu as pltpu
from jax.sharding import PartitionSpec as P

GELU_SCALE = 0.7978845608028654
BF = jnp.bfloat16
F32 = jnp.float32
MESH = pl.DeviceIdType.MESH

NI, NY, NC, NX, NZ = 4, 4, 2, 4, 2
NJ = NY * NC
RING = NZ * NI
ROWS, FEAT, BLOCK = 192, 96, 768
TOKENS = NI * ROWS
PACK, PR, PW = 4, 48, 384
NH = 3
HC = BLOCK // NH


def dot(left, right, contract):
    return lax.dot_general(left, right, (contract, ((), ())), preferred_element_type=F32)


NN = ((1,), (0,))
NT = ((1,), (1,))
TN = ((0,), (0,))


def guarded(when, action):
    if when is None:
        action()
    else:
        @pl.when(when)
        def _():
            action()


class Transfer:
    def __init__(self, copy, when, arrives):
        self.copy, self.when, self.arrives = copy, when, arrives

    def start(self):
        guarded(self.when, self.copy.start)

    def wait_send(self):
        guarded(self.when, self.copy.wait_send)

    def wait_recv(self):
        guarded(self.arrives, self.copy.wait_recv)


def kernel(
    feat_hbm, cot_hbm, w1_hbm, w2_hbm,
    out_ref, fgrad_ref, dw1_ref, dw2_ref,
    raw, own, gx, gc, xs, xt, cs, w1, w1r, w2, gpart, grecv, gpass, gsum, gz,
    ppart, precv, ppass, psum, pz,
    act, gp, dwb, dw2b,
    pk0, rc0, s0, ry0, t0, rz0, pk1, rc1, s1, ry1, t1, rz1,
    send_sem, recv_sem, local_sem,
):
    ia, ja, ka = lax.axis_index("ia"), lax.axis_index("ja"), lax.axis_index("ka")
    yy, cc, xx, zz = ja // NC, lax.rem(ja, NC), ka // NZ, lax.rem(ka, NZ)
    ring = zz * NI + ia

    def at_i(d):
        i = lax.rem(ia + d, NI)
        return i, (i, ja, ka)

    def at_z(d):
        z = lax.rem(ring + d, RING)
        return z, (lax.rem(z, NI), ja, xx * NZ + z // NI)

    def at_y(d):
        y = lax.rem(yy + d, NY)
        return y, (ia, y * NC + cc, ka)

    def at_x(x):
        return (ia, ja, x * NZ + zz)

    even, odd = xx + 1 - 2 * lax.rem(xx, 2), NX - 1 - xx
    first, second = even + cc * (odd - even), odd + cc * (even - odd)
    across = lax.rem(xx + 2, NX)

    core = (ia, yy * NC + 1 - cc, ka)
    zpair = at_z(NI)[1]

    barrier = pltpu.get_barrier_semaphore()
    peers = [at_z(d)[1] for d in range(1, RING)] + [at_y(d)[1] for d in (1, 2, 3)]
    peers += [at_x(first), at_x(second), core]
    for peer in peers:
        pl.semaphore_signal(barrier, inc=1, device_id=peer, device_id_type=MESH)

    count = [0, 0]
    sent = []

    def remote(src, dst, device, when=None, arrives=None):
        n = count[0]
        count[0] += 1
        copy = Transfer(pltpu.make_async_remote_copy(
            src_ref=src, dst_ref=dst, send_sem=send_sem.at[n], recv_sem=recv_sem.at[n],
            device_id=device, device_id_type=MESH,
        ), when, arrives)
        copy.start()
        sent.append(copy)
        return copy

    def nearby(src, dst):
        n = count[1]
        count[1] += 1
        copy = pltpu.make_async_copy(src, dst, local_sem.at[n])
        copy.start()
        return copy

    def cols(index, width):
        return pl.ds(pl.multiple_of(index * width, width), width)

    raw_copies = [nearby(cot_hbm, raw.at[0]), nearby(feat_hbm, raw.at[1])]
    w1_copy = nearby(w1_hbm, w1)
    w2_copy = nearby(w2_hbm, w2)
    for n in range(2):
        raw_copies[n].wait()
        own[n] = jnp.concatenate([raw[n, g * PR:(g + 1) * PR] for g in range(PACK)], axis=1)
    gc[ja, ia] = own[0]
    gx[ja, zz, ia] = own[1]
    pl.semaphore_wait(barrier, len(peers))

    odd_z = lax.rem(ia, 2)

    def high(y):
        near = lax.rem(y - ia + NI + 1, NI) - 1
        return lax.rem(ring + RING + near - NI * odd_z * ((near + 1) // 3), RING) // NI

    def in_reach(z, row):
        return lax.rem(row - z + 1 + lax.rem(z, 2) + RING, RING) <= 3

    def to_y(src, dst):
        return [remote(src, dst, at_y(d)[1]) for d in (1, 2, 3)]

    z_c = [remote(own.at[0], gc.at[ja, ia], at_i(d)[1]) for d in (1, 2, 3)]
    c_y = [to_y(own.at[0], gc.at[ja, ia])]
    for d, copy in zip((1, 2, 3), z_c):
        copy.wait_recv()
        i = lax.rem(ia + NI - d, NI)
        c_y.append(to_y(gc.at[ja, i], gc.at[ja, i]))
    c_core = [remote(gc.at[ja], gc.at[ja], core)]
    x_z = []
    for d in range(1, RING):
        z, device = at_z(d)
        source = lax.rem(ring + RING - d, RING)
        x_z.append(remote(
            own.at[1], gx.at[ja, zz, ia], device,
            in_reach(z, zz * NI + yy), in_reach(ring, source // NI * NI + yy),
        ))
    w1_copy.wait()
    w1_in = []
    for h in range(NH):
        w1_in.append([])
        for d in (1, 7, 6 - 4 * odd_z):
            z, device = at_z(d)
            place = cols(lax.rem(z, NI) * NH + h, HC)
            w1_in[h].append(remote(w1.at[:, place], w1r.at[h, cols(ia, ROWS)], device))
        w1r[h, cols(ia, ROWS)] = w1[:, cols(ia * NH + h, HC)]

    for d in (1, 2, 3):
        for copies in c_y:
            copies[d - 1].wait_recv()
        j = lax.rem(yy + NY - d, NY) * NC + cc
        c_core.append(remote(gc.at[j], gc.at[j], core))

    for copy in x_z:
        copy.wait_recv()
    here = high(yy)
    x_y = to_y(gx.at[ja, here], gx.at[ja, here])
    x_core = [remote(gx.at[ja, here], gx.at[ja, here], core)]

    def unpack(dst, rows_of):
        def body(i, carry):
            for g in range(PACK):
                row = pl.multiple_of(i * ROWS + g * PR, PR)
                dst[pl.ds(row, PR), :] = jnp.concatenate(
                    [rows_of(j, i)[:, g * FEAT:(g + 1) * FEAT] for j in range(NJ)], axis=1
                )
            return carry
        lax.fori_loop(0, NI, body, 0)

    for copy in c_core:
        copy.wait_recv()
    unpack(cs, lambda j, i: gc[j, i])
    w2_copy.wait()

    mine = cols(xx, ROWS)

    def sum_first(part, landing, h):
        return [
            remote(part.at[h, cols(x, ROWS)], landing.at[h, n], at_x(first))
            for n, x in ((1, across), (0, first))
        ]

    def sum_second(part, landing, passing, copies, h):
        copies[0].wait_recv()
        passing[h] = (part[h, cols(second, ROWS)].astype(F32) + landing[h, 1].astype(F32)).astype(BF)
        copies.append(remote(passing.at[h], landing.at[h, 2], at_x(second)))

    def sum_pair(part, landing, total_ref, other, copies, h):
        copies[1].wait_recv()
        copies[2].wait_recv()
        total = part[h, mine].astype(F32) + landing[h, 0].astype(F32) + landing[h, 2].astype(F32)
        total_ref[h] = total.astype(BF)
        return remote(total_ref.at[h], other.at[h], zpair)

    def grad_part(h):
        def body(t, carry):
            rows = cols(t, ROWS)
            gpart[h, rows] = dot(cs[rows], w2[h * HC:(h + 1) * HC], NT).astype(BF)
            return carry
        lax.fori_loop(0, NX, body, 0)
        return sum_first(gpart, grecv, h)

    g_x = [grad_part(h) for h in range(NH)]

    def grad_second(h):
        sum_second(gpart, grecv, gpass, g_x[h], h)

    def grad_pair(h):
        return sum_pair(gpart, grecv, gsum, gz, g_x[h], h)

    for d in (1, 2, 3):
        y = lax.rem(yy + NY - d, NY)
        x_y[d - 1].wait_recv()
        there = high(y)
        j = y * NC + cc
        x_core.append(remote(gx.at[j, there], gx.at[j, there], core))
    grad_second(0)
    for copy in x_core:
        copy.wait_recv()
    unpack(xs, lambda j, i: gx[j, high(j // NC), i])

    p_x = []
    for h in range(NH):
        for copy in w1_in[h]:
            copy.wait_recv()

        def body(t, carry):
            rows = cols(t, ROWS)
            ppart[h, rows] = dot(xs[rows], w1r[h], NN).astype(BF)
            return carry
        lax.fori_loop(0, NX, body, 0)
        p_x.append(sum_first(ppart, precv, h))
        if h < 2:
            grad_second(h + 1)
    g_z = [grad_pair(h) for h in range(NH)]

    def body(t, carry):
        xt[cols(t, 256)] = xs[:, cols(t, 256)].T
        return carry
    lax.fori_loop(0, BLOCK // 256, body, 0)

    p_z = []

    def pre_second(h):
        sum_second(ppart, precv, ppass, p_x[h], h)

    def pre_pair(h):
        p_z.append(sum_pair(ppart, precv, psum, pz, p_x[h], h))

    pre_second(0)
    pre_second(1)
    pre_pair(0)
    pre_second(2)
    pre_pair(1)
    pre_pair(2)

    class Gather:
        def __init__(self, ref, at):
            self.ref, self.at = ref, at
            self.own = [self.send(xx, x) for x in (first, second)]

        def send(self, rows, x):
            piece = self.ref.at[self.at, cols(rows, ROWS)]
            return remote(piece, piece, at_x(x))

        def pass_on(self):
            self.own[0].wait_recv()
            self.own.append(self.send(first, second))

        def finish(self):
            for copy in self.own[1:]:
                copy.wait_recv()

    gp_x, act_x = [], []

    def activate(h):
        p_z[h].wait_recv()
        pre = psum[h].astype(F32) + pz[h].astype(F32)
        square = pre * pre
        tangent = jnp.tanh(GELU_SCALE * (pre + 0.044715 * square * pre))
        act[h, mine] = (0.5 * pre * (1.0 + tangent)).astype(BF)
        slope = 0.5 * (1.0 + tangent) + 0.5 * pre * (1.0 - tangent * tangent) * GELU_SCALE * (
            1.0 + 3.0 * 0.044715 * square
        )
        g_z[h].wait_recv()
        grad = gsum[h].astype(F32) + gz[h].astype(F32)
        gp[h, mine] = (grad * slope).astype(BF)
        gp_x.append(Gather(gp, h))

    dw1_in, dw1_own = [], []

    def in_weight_grad(h):
        def body(t, carry):
            dwb[h, cols(t, 256)] = dot(xt[cols(t, 256)], gp[h], NN).astype(BF)
            return carry
        lax.fori_loop(0, BLOCK // 256, body, 0)
        place = cols(ia * NH + h, HC)
        for d in (1, 7, 2 + 4 * odd_z):
            z, device = at_z(d)
            dw1_in.append(remote(dwb.at[h, cols(lax.rem(z, NI), ROWS)], dw1_ref.at[:, place], device))
        dw1_own.append(nearby(dwb.at[h, cols(ia, ROWS)], dw1_ref.at[:, place]))

    activate(0)
    activate(1)
    gp_x[0].pass_on()
    activate(2)
    gp_x[1].pass_on()
    act_x += [Gather(act, 0), Gather(act, 1)]
    gp_x[2].pass_on()
    act_x.append(Gather(act, 2))
    act_x[0].pass_on()
    act_x[1].pass_on()
    gp_x[0].finish()
    in_weight_grad(0)
    gp_x[1].finish()
    gp_x[2].finish()
    act_x[2].pass_on()

    def packed(value, j):
        return jnp.concatenate(
            [value[g * PR:(g + 1) * PR, j * FEAT:(j + 1) * FEAT] for g in range(PACK)], axis=1
        )

    def body(i, carry):
        rows = cols(i, ROWS)
        left = jnp.concatenate([gp[h, rows] for h in range(NH)], axis=1)
        right = jnp.concatenate([w1r[h] for h in range(NH)], axis=1)
        total = dot(left, right, NT).astype(BF)
        for j in range(NJ):
            pk0[j, i] = packed(total, j)
        return carry
    lax.fori_loop(0, NI, body, 0)
    def to_core(part, landing):
        copies = []
        for d in range(NY):
            y = lax.rem(yy + d, NY)
            copies.append(remote(part.at[y * NC + 1 - cc], landing.at[y], core))
        return copies

    core0 = to_core(pk0, rc0)
    in_weight_grad(1)

    def to_rows(partial, arrived, copies, summed, landing):
        started = []
        for d in (1, 2, 3, 0):
            y, device = at_y(d)
            copies[d].wait_recv()
            summed[y] = (partial[y * NC + cc].astype(F32) + arrived[y].astype(F32)).astype(BF)
            if d:
                started.append(remote(summed.at[y], landing.at[d - 1], device))
        return started

    y0 = to_rows(pk0, rc0, core0, s0, ry0)

    for gather in act_x:
        gather.finish()

    def body(i, carry):
        rows = cols(i, ROWS)
        left = jnp.concatenate([act[h, rows] for h in range(NH)], axis=1)
        total = dot(left, w2[...], NN).astype(BF)
        for j in range(NJ):
            pk1[j, i] = packed(total, j)
        return carry
    lax.fori_loop(0, NI, body, 0)
    core1 = to_core(pk1, rc1)
    in_weight_grad(2)
    y1 = to_rows(pk1, rc1, core1, s1, ry1)

    for copy in y0:
        copy.wait_recv()
    total = s0[yy].astype(F32)
    for d in range(3):
        total += ry0[d].astype(F32)
    t0[...] = total.astype(BF)
    z0 = []
    for d in range(1, RING):
        z, device = at_z(d)
        source = lax.rem(ring + RING - d, RING)
        z0.append(remote(
            t0.at[lax.rem(z, NI)], rz0.at[d - 1], device,
            in_reach(ring, z // NI * NI + yy), in_reach(source, zz * NI + yy),
        ))

    for h in range(NH):
        dw2b[h * HC:(h + 1) * HC] = dot(act[h], cs[...], TN).astype(BF)
    dw2_copy = nearby(dw2b, dw2_ref)

    for copy in y1:
        copy.wait_recv()
    total = s1[yy].astype(F32)
    for d in range(3):
        total += ry1[d].astype(F32)
    t1[...] = total.astype(BF)
    z1 = []
    for d in (1, 2, 3):
        i, device = at_i(d)
        z1.append(remote(t1.at[i], rz1.at[d - 1], device))

    def finish(total, ref):
        total = total.astype(BF)
        for g in range(PACK):
            ref[g * PR:(g + 1) * PR, :] = total[:, g * FEAT:(g + 1) * FEAT]

    total = jnp.where(here == zz, t0[ia].astype(F32), 0.0)
    for n, copy in enumerate(z0):
        copy.wait_recv()

        @pl.when(jnp.logical_not(copy.arrives))
        def _():
            rz0[n] = jnp.zeros((PR, PW), BF)
        total += rz0[n].astype(F32)
    finish(total, fgrad_ref)

    total = t1[ia].astype(F32)
    for n, copy in enumerate(z1):
        copy.wait_recv()
        total += rz1[n].astype(F32)
    finish(total, out_ref)

    for copy in dw1_in:
        copy.wait_recv()
    for copy in dw1_own + [dw2_copy]:
        copy.wait()
    for copy in sent:
        copy.wait_send()


def handover(*refs):
    sources, targets, staging, sem = refs[:4], refs[4:8], refs[8:12], refs[12]
    pieces = []
    for source, stage, target in zip(sources, staging, targets):
        parts = 4 if source.shape[1] > BLOCK // 2 else 1
        rows = source.shape[0] // parts
        for n in range(parts):
            at = pl.ds(n * rows, rows)
            pieces.append((source.at[at], stage.at[at], target.at[at]))
    loads = [pltpu.make_async_copy(p[0], p[1], sem.at[0, n]) for n, p in enumerate(pieces)]
    stores = [pltpu.make_async_copy(p[1], p[2], sem.at[1, n]) for n, p in enumerate(pieces)]
    for load in loads:
        load.start()
    for load, store in zip(loads, stores):
        load.wait()
        store.start()
    for store in stores:
        store.wait()


def local(features, in_weight, out_weight, cotangent):
    vmem = pl.BlockSpec(memory_space=pltpu.VMEM)
    hbm = pl.BlockSpec(memory_space=pl.ANY)
    buf = lambda *shape: pltpu.VMEM(shape, BF)
    wide = lambda *shape: pltpu.VMEM(shape, F32)
    results = pl.pallas_call(
        kernel,
        out_shape=(
            jax.ShapeDtypeStruct((ROWS, FEAT), BF),
            jax.ShapeDtypeStruct((ROWS, FEAT), BF),
            jax.ShapeDtypeStruct((ROWS, NI * BLOCK), BF),
            jax.ShapeDtypeStruct((BLOCK, BLOCK), BF),
        ),
        in_specs=[hbm] * 4,
        out_specs=(vmem, vmem, hbm, hbm),
        scratch_shapes=[
            buf(2, ROWS, FEAT), buf(2, PR, PW), buf(NJ, NZ, NI, PR, PW), buf(NJ, NI, PR, PW),
            buf(TOKENS, BLOCK), buf(BLOCK, TOKENS), buf(TOKENS, BLOCK),
            buf(ROWS, NI * BLOCK), buf(NH, BLOCK, HC), buf(BLOCK, BLOCK),
            buf(NH, TOKENS, HC), buf(NH, 3, ROWS, HC), buf(NH, ROWS, HC),
            buf(NH, ROWS, HC), buf(NH, ROWS, HC),
            buf(NH, TOKENS, HC), buf(NH, 3, ROWS, HC), buf(NH, ROWS, HC),
            buf(NH, ROWS, HC), buf(NH, ROWS, HC),
            buf(NH, TOKENS, HC), buf(NH, TOKENS, HC),
            buf(NH, BLOCK, HC), buf(BLOCK, BLOCK),
            buf(NJ, NI, PR, PW), buf(NY, NI, PR, PW), buf(NY, NI, PR, PW),
            buf(3, NI, PR, PW), buf(NI, PR, PW), buf(RING - 1, PR, PW),
            buf(NJ, NI, PR, PW), buf(NY, NI, PR, PW), buf(NY, NI, PR, PW),
            buf(3, NI, PR, PW), buf(NI, PR, PW), buf(3, PR, PW),
            pltpu.SemaphoreType.DMA((118,)),
            pltpu.SemaphoreType.DMA((118,)),
            pltpu.SemaphoreType.DMA((8,)),
        ],
        name="block",
        compiler_params=pltpu.CompilerParams(
            collective_id=0, has_side_effects=True, vmem_limit_bytes=60 * 2**20
        ),
        cost_estimate=pl.CostEstimate(
            flops=12 * BLOCK**3, bytes_accessed=8 * BLOCK * BLOCK, transcendentals=ROWS * BLOCK
        ),
    )(features, cotangent, in_weight, out_weight)
    return pl.pallas_call(
        handover,
        out_shape=tuple(jax.ShapeDtypeStruct(r.shape, r.dtype) for r in results),
        in_specs=[hbm] * 4,
        out_specs=(hbm,) * 4,
        scratch_shapes=[pltpu.VMEM(r.shape, r.dtype) for r in results] + [pltpu.SemaphoreType.DMA((2, 10))],
        name="handover",
        compiler_params=pltpu.CompilerParams(vmem_limit_bytes=60 * 2**20),
    )(*results)


def solution(mesh):
    placed = (
        P("ia", ("ka", "ja")),
        P(("ka", "ia"), "ja"),
        P(("ja", "ia"), "ka"),
        P("ia", ("ka", "ja")),
    )
    return jax.shard_map(
        local,
        mesh=mesh,
        in_specs=placed,
        out_specs=(
            P("ia", ("ka", "ja")),
            P("ia", ("ka", "ja")),
            P(("ka", "ia"), "ja"),
            P(("ja", "ia"), "ka"),
        ),
        check_vma=False,
    )
```
